32 devices in a mesh: grp: 4 (over y, x), aux: 8 (over z, core).
Axes of the slice: x: 2, y: 2, z: 4, core: 2. Of those that a mesh axis runs over, the one named last changes fastest.
Arguments:
- integrals: bfloat16 [2048, 32, 512], P('aux', 'grp'), may hold values from -0.75 to 0.75
- metric: bfloat16 [2048, 2048], replicated, may hold values from -0.125 to 0.125
- occupied_energy: float32 [32], replicated, may hold values from -2 to -0.5
- virtual_energy: float32 [512], replicated, may hold values from 0.2 to 3
- plan: int32 [4, 8], replicated, may hold values from 0 to 3
Outputs:
- density: bfloat16 [2048, 32, 512], P('aux', 'grp')
The draws below stay inside these ranges and needn't reach their ends.
All inputs are finite; a program needn't handle non-finite values.
Results may differ from the reference program's by a relative error of at most 0.0053.
Values may be sent and summed in bfloat16 or wider, within the bound.
A program may use at most 128 MiB of HBM per device.

```python
import math
import jax
import jax.numpy as jnp
from jax import lax

NVIRT = 512
NAUX = 2048
OCC_DEV = 1
STEPS = 4
OCC_GRP = 8
NOCC = 32
N_GRP = 4
N_AUX = 8


def with_ends(result, own_key, low, high):
    longest = result.shape.index(max(result.shape))
    spots = []
    for shift in (0, 1):
        where = [jax.random.randint(jax.random.fold_in(own_key, axis), (), 0, length) for axis, length in enumerate(result.shape)]
        where[longest] = (where[longest] + shift) % result.shape[longest]
        spots.append(tuple(where))
    return result.at[spots[0]].set(low).at[spots[1]].set(high)


def steps_of(stream_key, shape, split, least, high):
    gain = 1.0
    for dim, blocks in split:
        draws = jax.random.uniform(jax.random.fold_in(jax.random.fold_in(stream_key, 6), dim), (blocks,), jnp.float32, least / len(split), high / len(split))
        gain = gain * jnp.repeat(jnp.exp(draws), shape[dim] // blocks).reshape((-1,) + (1,) * (len(shape) - 1 - dim))
    return gain


def centred(own_key, shape, width, bound, pieces=(), held_as=jnp.bfloat16):
    entries = width * jax.random.normal(own_key, shape, jnp.float32)
    if pieces:
        entries = entries * steps_of(own_key, shape, pieces, -0.22, 0.18)
    return jnp.clip(entries, -bound, bound).astype(held_as)


def setup_inputs(seed: int = 0) -> dict:
    seeds = jax.random.split(jax.random.key(seed), 6)
    return {
        "integrals": centred(seeds[0], (NAUX, NOCC, NVIRT), 0.12, 0.75, ((0, 8), (1, 4))),
        "metric": centred(seeds[1], (NAUX, NAUX), NAUX ** -0.5, 0.125),
        "occupied_energy": jnp.clip(jax.random.uniform(seeds[2], (NOCC,), jnp.float32, -2.0, -0.5), -2.0, -0.5),
        "virtual_energy": jnp.clip(jnp.exp(jax.random.uniform(seeds[3], (NVIRT,), jnp.float32, math.log(0.2), math.log(3.0))), 0.2, 3.0),
        "plan": with_ends(jax.random.randint(seeds[4], (STEPS, N_AUX), 0, N_GRP), jax.random.fold_in(seeds[4], 1), 0, N_GRP - 1).astype(jnp.int32),
    }


def pair_term(own_block, partner, own_energy, partner_energy, virtual_energy):
    coulomb = jnp.einsum('qia,qjb->ijab', own_block.astype(jnp.float32), partner.astype(jnp.float32))
    denominator = (own_energy[:, None, None, None] + partner_energy[None, :, None, None]
                   - virtual_energy[None, None, :, None] - virtual_energy[None, None, None, :])
    amplitude = ((2.0 * coulomb - jnp.swapaxes(coulomb, 2, 3)) / denominator).astype(jnp.bfloat16)
    return jnp.einsum('ijab,qjb->qia', amplitude.astype(jnp.float32), partner.astype(jnp.float32))


def reference(integrals, metric, occupied_energy, virtual_energy, plan):
    metric_wide = metric.astype(jnp.float32)

    def transform(group_index):
        slab_rows = lax.dynamic_slice_in_dim(integrals, group_index * OCC_GRP, OCC_GRP, 1)
        product = jnp.dot(metric_wide, slab_rows.reshape(NAUX, OCC_GRP * NVIRT).astype(jnp.float32))
        product = product.astype(jnp.bfloat16).reshape(NAUX, N_AUX, OCC_DEV, NVIRT)
        return jnp.moveaxis(product, 1, 0)

    coeff = lax.map(transform, jnp.arange(N_GRP, dtype=jnp.int32))
    coeff = coeff.reshape(N_GRP * N_AUX, NAUX, OCC_DEV, NVIRT)

    def pair_block(block_index):
        own_block = lax.dynamic_index_in_dim(coeff, block_index, 0, keepdims=False)
        aux_place = (block_index % N_AUX).astype(jnp.int32)
        own_energy = lax.dynamic_slice_in_dim(occupied_energy, block_index * OCC_DEV, OCC_DEV)
        density_sum = jnp.zeros((NAUX, OCC_DEV, NVIRT), jnp.float32)
        for step_index in range(STEPS):
            owner_group = lax.dynamic_index_in_dim(plan[step_index], aux_place, 0, keepdims=False)
            partner_index = (owner_group * N_AUX + aux_place).astype(jnp.int32)
            partner = lax.dynamic_index_in_dim(coeff, partner_index, 0, keepdims=False)
            partner_energy = lax.dynamic_slice_in_dim(occupied_energy, partner_index * OCC_DEV, OCC_DEV)
            density_sum = density_sum + pair_term(own_block, partner, own_energy, partner_energy, virtual_energy)
        return density_sum.astype(jnp.bfloat16)

    density = lax.map(pair_block, jnp.arange(N_GRP * N_AUX, dtype=jnp.int32))
    return jnp.moveaxis(density, 0, 1).reshape(NAUX, NOCC, NVIRT)
```

```python
import functools

import jax
import jax.numpy as jnp
from jax import lax
from jax.experimental import pallas as pl
from jax.experimental.pallas import tpu as pltpu
from jax.sharding import PartitionSpec as P

MESH = pl.DeviceIdType.MESH
CHUNK = 128


def dot(left, right):
    return lax.dot_general(left, right, (((1,), (0,)), ((), ())), preferred_element_type=jnp.float32)


def kernel(n, shards, x, metric, vrow, vcol, occ, plan, y, mvm, recv, blocks, own_t, exch, amp, dens,
           msem, in_send, in_recv, in_local, g_send, g_recv, f_send, f_recv, out_send, out_recv, out_local):
    grp = lax.axis_index("grp")
    me = lax.axis_index("aux")
    chunks, rows, width = x.shape[1], x.shape[2], x.shape[3]
    aux_rows = metric.shape[0]
    nvirt = vrow.shape[1]
    relay = n == 4
    steps = plan.shape[0]

    def aux_at(d):
        return lax.rem(me + d, shards)

    if relay:
        one = grp + 1 - 2 * lax.rem(grp, 2)
        two = lax.rem(grp + 2, 4)
        target = [grp, one, two, lax.rem(one + 2, 4)]
        source = target
    else:
        target = [lax.rem(grp + d, n) for d in range(n)]
        source = [lax.rem(grp + n - d, n) for d in range(n)]

    load = pltpu.make_async_copy(metric, mvm, msem)
    load.start()

    barrier = pltpu.get_barrier_semaphore()

    @pl.loop(1, shards)
    def _(d):
        pl.semaphore_signal(barrier, inc=1, device_id=(grp, aux_at(d)), device_id_type=MESH)

    for d in range(1, n):
        pl.semaphore_signal(barrier, inc=1, device_id=(target[d], me), device_id_type=MESH)
    pl.semaphore_wait(barrier, shards - 1 + n - 1)

    def in_copy(k, d):
        return pltpu.make_async_remote_copy(
            src_ref=x.at[aux_at(d), k], dst_ref=recv.at[k, me], send_sem=in_send.at[k, d],
            recv_sem=in_recv.at[k, d], device_id=(grp, aux_at(d)), device_id_type=MESH)

    def in_own(k):
        return pltpu.make_async_copy(x.at[me, k], recv.at[k, me], in_local.at[k])

    def send_in(k):
        in_own(k).start()

        @pl.loop(1, shards)
        def _(d):
            in_copy(k, d).start()

    def wait_in(k):
        in_own(k).wait()

        @pl.loop(1, shards)
        def _(d):
            place = lax.rem(me + shards - d, shards)
            pltpu.make_async_remote_copy(
                src_ref=x.at[place, k], dst_ref=recv.at[k, place], send_sem=in_send.at[k, d],
                recv_sem=in_recv.at[k, d], device_id=(grp, aux_at(d)), device_id_type=MESH).wait_recv()

    def g_copy(k, d):
        return pltpu.make_async_remote_copy(
            src_ref=blocks.at[0, k], dst_ref=blocks.at[d, k], send_sem=g_send.at[d, k],
            recv_sem=g_recv.at[d, k], device_id=(target[d], me), device_id_type=MESH)

    half = aux_rows // 2

    def f_copy(k, way):
        part = pl.ds(way * half, half)
        return pltpu.make_async_remote_copy(
            src_ref=blocks.at[1 + way, k, part], dst_ref=blocks.at[3, k, part], send_sem=f_send.at[way, k],
            recv_sem=f_recv.at[way, k], device_id=(target[2 - way], me), device_id_type=MESH)

    direct = (1, 2) if relay else tuple(range(1, n))

    def forward(k):
        for d in (1, 2):
            g_copy(k, d).wait_recv()
            f_copy(k, d - 1).start()

    tile = min(512, aux_rows)
    send_in(0)
    if chunks > 1:
        send_in(1)
    for k in range(chunks):
        wait_in(k)
        if k + 2 < chunks:
            send_in(k + 2)
        if k == 0:
            load.wait()

        @pl.loop(0, aux_rows // tile)
        def _(t):
            at = pl.ds(pl.multiple_of(t * tile, tile), tile)
            part = dot(mvm[at, :], recv[k].reshape(aux_rows, width))
            blocks[0, k, at, :] = part.astype(jnp.bfloat16)

        for d in direct:
            g_copy(k, d).start()
        if relay and k >= 1:
            forward(k - 1)
        own_t[k * width:(k + 1) * width, :] = blocks[0, k].T

    def pair(d):
        per = max(1, min(256 // width, chunks))
        for k in range(0, chunks, per):
            right = jnp.concatenate([blocks[d, k + m] for m in range(per)], axis=1)
            exch[:, k * width:(k + per) * width] = dot(own_t[...], right)
        weight = jnp.float32(0.0)
        for s in range(steps):
            weight = weight + jnp.where(plan[s, me] == source[d], jnp.float32(1.0), jnp.float32(0.0))
        shift = occ[grp * shards + me] + occ[source[d] * shards + me]
        value = exch[...]
        below = shift - vcol[...] - vrow[...]
        value = weight * ((2.0 * value.T - value) / below)
        amp[d * nvirt:(d + 1) * nvirt, :] = value.astype(jnp.bfloat16)

    pair(0)
    if relay:
        forward(chunks - 1)
        pair(1)
        pair(2)
        for k in range(chunks):
            for way in (0, 1):
                f_copy(k, way).wait_recv()
        pair(3)
    else:
        for d in direct:
            for k in range(chunks):
                g_copy(k, d).wait_recv()
            pair(d)

    def density(d):
        at = pl.ds(pl.multiple_of(aux_at(d) * rows, rows), rows)
        left = jnp.concatenate([blocks[s, k, at, :] for s in range(n) for k in range(chunks)], axis=1)
        dens[d] = dot(left, amp[...]).astype(jnp.bfloat16)

    def out_copy(d):
        return pltpu.make_async_remote_copy(
            src_ref=dens.at[d], dst_ref=y.at[me], send_sem=out_send.at[d], recv_sem=out_recv.at[d],
            device_id=(grp, aux_at(d)), device_id_type=MESH)

    @pl.loop(1, shards)
    def _(d):
        density(d)
        out_copy(d).start()

    density(0)
    own_out = pltpu.make_async_copy(dens.at[0], y.at[me], out_local)
    own_out.start()
    own_out.wait()

    for k in range(chunks):
        @pl.loop(1, shards)
        def _(d):
            in_copy(k, d).wait_send()

        for d in direct:
            g_copy(k, d).wait_send()
        if relay:
            for way in (0, 1):
                f_copy(k, way).wait_send()

    @pl.loop(1, shards)
    def _(d):
        place = lax.rem(me + shards - d, shards)
        out_copy(d).wait_send()
        pltpu.make_async_remote_copy(
            src_ref=dens.at[d], dst_ref=y.at[place], send_sem=out_send.at[d], recv_sem=out_recv.at[d],
            device_id=(grp, aux_at(d)), device_id_type=MESH).wait_recv()


def body(integrals, metric, occupied_energy, virtual_energy, plan):
    n, shards = lax.axis_size("grp"), lax.axis_size("aux")
    rows, places, nvirt = integrals.shape
    aux_rows = metric.shape[0]
    width = CHUNK if nvirt % CHUNK == 0 else nvirt
    chunks = nvirt // width
    x = integrals.reshape(rows, shards, chunks, width).transpose(1, 2, 0, 3)
    any_space = pl.BlockSpec(memory_space=pl.ANY)
    vmem = pl.BlockSpec(memory_space=pltpu.VMEM)
    smem = pl.BlockSpec(memory_space=pltpu.SMEM)
    dma = pltpu.SemaphoreType.DMA
    flops = 2 * aux_rows * nvirt * (aux_rows + 2 * n * nvirt)
    y = pl.pallas_call(
        functools.partial(kernel, n, shards),
        out_shape=jax.ShapeDtypeStruct((shards, rows, nvirt), jnp.bfloat16),
        in_specs=[any_space, any_space, vmem, vmem, smem, smem],
        out_specs=any_space,
        scratch_shapes=[
            pltpu.VMEM((aux_rows, aux_rows), jnp.bfloat16),
            pltpu.VMEM((chunks, shards, rows, width), jnp.bfloat16),
            pltpu.VMEM((n, chunks, aux_rows, width), jnp.bfloat16),
            pltpu.VMEM((nvirt, aux_rows), jnp.bfloat16),
            pltpu.VMEM((nvirt, nvirt), jnp.float32),
            pltpu.VMEM((n * nvirt, nvirt), jnp.bfloat16),
            pltpu.VMEM((shards, rows, nvirt), jnp.bfloat16),
            dma, dma((chunks, shards)), dma((chunks, shards)), dma((chunks,)),
            dma((n, chunks)), dma((n, chunks)), dma((2, chunks)), dma((2, chunks)),
            dma((shards,)), dma((shards,)), dma,
        ],
        compiler_params=pltpu.CompilerParams(
            collective_id=0, has_side_effects=True, vmem_limit_bytes=56 * 1024 * 1024),
        cost_estimate=pl.CostEstimate(
            flops=flops, bytes_accessed=2 * aux_rows * aux_rows, transcendentals=0),
    )(x, metric, virtual_energy.reshape(1, nvirt), virtual_energy.reshape(nvirt, 1), occupied_energy, plan)
    return y.transpose(1, 0, 2)


def solution(mesh):
    in_specs = (P("aux", "grp", None), P(), P(), P(), P())
    out_specs = P("aux", "grp", None)
    return jax.shard_map(body, mesh=mesh, in_specs=in_specs, out_specs=out_specs, check_vma=False)
```

```python
import functools

import jax
import jax.numpy as jnp
from jax import lax
from jax.experimental import pallas as pl
from jax.experimental.pallas import tpu as pltpu
from jax.sharding import PartitionSpec as P

MESH = pl.DeviceIdType.MESH
CHUNK = 128
WINDOW = 3


def dot(left, right):
    return lax.dot_general(left, right, (((1,), (0,)), ((), ())), preferred_element_type=jnp.float32)


def kernel(n, shards, x, metric, vrow, occ, plan, y, mvm, recv, blocks, own_t, exch, vsum, amp, dens,
           msem, in_send, in_recv, in_local, g_send, g_recv, f_send, f_recv, out_send, out_recv, out_local):
    grp = lax.axis_index("grp")
    me = lax.axis_index("aux")
    chunks, rows, width = x.shape[1], x.shape[2], x.shape[3]
    aux_rows = metric.shape[0]
    nvirt = vrow.shape[1]
    relay = n == 4
    steps = plan.shape[0]

    def aux_at(d):
        return lax.rem(me + d, shards)

    if relay:
        one = grp + 1 - 2 * lax.rem(grp, 2)
        two = lax.rem(grp + 2, 4)
        target = [grp, one, two, lax.rem(one + 2, 4)]
        source = target
    else:
        target = [lax.rem(grp + d, n) for d in range(n)]
        source = [lax.rem(grp + n - d, n) for d in range(n)]

    load = pltpu.make_async_copy(metric, mvm, msem)
    load.start()

    barrier = pltpu.get_barrier_semaphore()

    @pl.loop(1, shards)
    def _(d):
        pl.semaphore_signal(barrier, inc=1, device_id=(grp, aux_at(d)), device_id_type=MESH)

    for d in range(1, n):
        pl.semaphore_signal(barrier, inc=1, device_id=(target[d], me), device_id_type=MESH)
    pl.semaphore_wait(barrier, shards - 1 + n - 1)

    def in_copy(k, d):
        return pltpu.make_async_remote_copy(
            src_ref=x.at[aux_at(d), k], dst_ref=recv.at[k, me], send_sem=in_send.at[k, d],
            recv_sem=in_recv.at[k, d], device_id=(grp, aux_at(d)), device_id_type=MESH)

    def in_own(k):
        return pltpu.make_async_copy(x.at[me, k], recv.at[k, me], in_local.at[k])

    parity = lax.rem(me, 2)
    per_class = shards // 2

    def class_loop(odd, act):
        @pl.loop(0, per_class)
        def _(e):
            d = 2 * lax.rem(e + per_class // 2, per_class) + (1 - parity if odd else parity)

            @pl.when(d != 0)
            def _():
                act(d)

    def send_step(i):
        class_loop(i // chunks, lambda d: in_copy(i % chunks, d).start())

    def send_after(k):
        class_loop(0, lambda d: in_copy(k, d).wait_send())
        for i in range(k + WINDOW, 2 * chunks if k == chunks - 1 else k + WINDOW + 1):
            send_step(i)

    def wait_in(k):
        in_own(k).wait()

        @pl.loop(1, shards)
        def _(d):
            place = lax.rem(me + shards - d, shards)
            pltpu.make_async_remote_copy(
                src_ref=x.at[place, k], dst_ref=recv.at[k, place], send_sem=in_send.at[k, d],
                recv_sem=in_recv.at[k, d], device_id=(grp, aux_at(d)), device_id_type=MESH).wait_recv()

    def g_copy(k, d):
        return pltpu.make_async_remote_copy(
            src_ref=blocks.at[0, k], dst_ref=blocks.at[d, k], send_sem=g_send.at[d, k],
            recv_sem=g_recv.at[d, k], device_id=(target[d], me), device_id_type=MESH)

    half = aux_rows // 2

    def f_copy(k, way):
        part = pl.ds(way * half, half)
        return pltpu.make_async_remote_copy(
            src_ref=blocks.at[1 + way, k, part], dst_ref=blocks.at[3, k, part], send_sem=f_send.at[way, k],
            recv_sem=f_recv.at[way, k], device_id=(target[2 - way], me), device_id_type=MESH)

    direct = (1, 2) if relay else tuple(range(1, n))

    def forward(k):
        for d in (1, 2):
            g_copy(k, d).wait_recv()
            f_copy(k, d - 1).start()

    tile = min(512, aux_rows)
    for k in range(chunks):
        in_own(k).start()
    for i in range(WINDOW):
        send_step(i)
    vsum[...] = vrow[...] + jnp.broadcast_to(vrow[...], (nvirt, nvirt)).T

    @pl.when(parity == 1)
    def _():
        for k in range(chunks):
            send_after(k)

    for k in range(chunks):
        wait_in(k)

        @pl.when(parity == 0)
        def _():
            send_after(k)

        if k == 0:
            load.wait()

        @pl.loop(0, aux_rows // tile)
        def _(t):
            at = pl.ds(pl.multiple_of(t * tile, tile), tile)
            part = dot(mvm[at, :], recv[k].reshape(aux_rows, width))
            blocks[0, k, at, :] = part.astype(jnp.bfloat16)

        for d in direct:
            g_copy(k, d).start()
        if relay and k >= 1:
            forward(k - 1)
        own_t[k * width:(k + 1) * width, :] = blocks[0, k].T

    def pair(d):
        per = max(1, min(256 // width, chunks))
        for k in range(0, chunks, per):
            right = jnp.concatenate([blocks[d, k + m] for m in range(per)], axis=1)
            exch[:, k * width:(k + per) * width] = dot(own_t[...], right)
        weight = jnp.float32(0.0)
        for s in range(steps):
            weight = weight + jnp.where(plan[s, me] == source[d], jnp.float32(1.0), jnp.float32(0.0))
        shift = occ[grp * shards + me] + occ[source[d] * shards + me]
        value = exch[...]
        below = shift - vsum[...]
        value = weight * ((2.0 * value.T - value) / below)
        amp[d * nvirt:(d + 1) * nvirt, :] = value.astype(jnp.bfloat16)

    pair(0)
    if relay:
        forward(chunks - 1)
        pair(1)
        pair(2)
        for k in range(chunks):
            for way in (0, 1):
                f_copy(k, way).wait_recv()
        pair(3)
    else:
        for d in direct:
            for k in range(chunks):
                g_copy(k, d).wait_recv()
            pair(d)

    def density(d):
        at = pl.ds(pl.multiple_of(aux_at(d) * rows, rows), rows)
        left = jnp.concatenate([blocks[s, k, at, :] for s in range(n) for k in range(chunks)], axis=1)
        dens[d] = dot(left, amp[...]).astype(jnp.bfloat16)

    def out_copy(d):
        return pltpu.make_async_remote_copy(
            src_ref=dens.at[d], dst_ref=y.at[me], send_sem=out_send.at[d], recv_sem=out_recv.at[d],
            device_id=(grp, aux_at(d)), device_id_type=MESH)

    @pl.loop(0, shards - 1)
    def _(t):
        d = 1 + lax.rem(t + shards // 2 - 1, shards - 1)
        density(d)
        out_copy(d).start()

    density(0)
    own_out = pltpu.make_async_copy(dens.at[0], y.at[me], out_local)
    own_out.start()
    own_out.wait()

    for k in range(chunks):
        class_loop(1, lambda d: in_copy(k, d).wait_send())
        for d in direct:
            g_copy(k, d).wait_send()
        if relay:
            for way in (0, 1):
                f_copy(k, way).wait_send()

    @pl.loop(1, shards)
    def _(d):
        place = lax.rem(me + shards - d, shards)
        out_copy(d).wait_send()
        pltpu.make_async_remote_copy(
            src_ref=dens.at[d], dst_ref=y.at[place], send_sem=out_send.at[d], recv_sem=out_recv.at[d],
            device_id=(grp, aux_at(d)), device_id_type=MESH).wait_recv()


def body(integrals, metric, occupied_energy, virtual_energy, plan):
    n, shards = lax.axis_size("grp"), lax.axis_size("aux")
    rows, places, nvirt = integrals.shape
    aux_rows = metric.shape[0]
    width = CHUNK if nvirt % CHUNK == 0 else nvirt
    chunks = nvirt // width
    x = integrals.reshape(rows, shards, chunks, width).transpose(1, 2, 0, 3)
    any_space = pl.BlockSpec(memory_space=pl.ANY)
    vmem = pl.BlockSpec(memory_space=pltpu.VMEM)
    smem = pl.BlockSpec(memory_space=pltpu.SMEM)
    dma = pltpu.SemaphoreType.DMA
    flops = 2 * aux_rows * nvirt * (aux_rows + 2 * n * nvirt)
    y = pl.pallas_call(
        functools.partial(kernel, n, shards),
        out_shape=jax.ShapeDtypeStruct((shards, rows, nvirt), jnp.bfloat16),
        in_specs=[any_space, any_space, vmem, smem, smem],
        out_specs=any_space,
        scratch_shapes=[
            pltpu.VMEM((aux_rows, aux_rows), jnp.bfloat16),
            pltpu.VMEM((chunks, shards, rows, width), jnp.bfloat16),
            pltpu.VMEM((n, chunks, aux_rows, width), jnp.bfloat16),
            pltpu.VMEM((nvirt, aux_rows), jnp.bfloat16),
            pltpu.VMEM((nvirt, nvirt), jnp.float32),
            pltpu.VMEM((nvirt, nvirt), jnp.float32),
            pltpu.VMEM((n * nvirt, nvirt), jnp.bfloat16),
            pltpu.VMEM((shards, rows, nvirt), jnp.bfloat16),
            dma, dma((chunks, shards)), dma((chunks, shards)), dma((chunks,)),
            dma((n, chunks)), dma((n, chunks)), dma((2, chunks)), dma((2, chunks)),
            dma((shards,)), dma((shards,)), dma,
        ],
        compiler_params=pltpu.CompilerParams(
            collective_id=0, has_side_effects=True, vmem_limit_bytes=56 * 1024 * 1024),
        cost_estimate=pl.CostEstimate(
            flops=flops, bytes_accessed=2 * aux_rows * aux_rows, transcendentals=0),
    )(x, metric, virtual_energy.reshape(1, nvirt), occupied_energy, plan)
    return y.transpose(1, 0, 2)


def solution(mesh):
    in_specs = (P("aux", "grp", None), P(), P(), P(), P())
    out_specs = P("aux", "grp", None)
    return jax.shard_map(body, mesh=mesh, in_specs=in_specs, out_specs=out_specs, check_vma=False)
```

```python
import functools

import jax
import jax.numpy as jnp
from jax import lax
from jax.experimental import pallas as pl
from jax.experimental.pallas import tpu as pltpu
from jax.sharding import PartitionSpec as P

MESH = pl.DeviceIdType.MESH
CHUNK = 128
WINDOW = 3


def dot(left, right):
    return lax.dot_general(left, right, (((1,), (0,)), ((), ())), preferred_element_type=jnp.float32)


def kernel(n, shards, width, raw, metric, vrow, occ, plan, y, held, x, mvm, recv, blocks, own_t, exch, vsum, amp, dens,
           msem, raw_sem, in_send, in_recv, in_local, g_send, g_recv, f_send, f_recv, out_send, out_recv, out_local):
    grp = lax.axis_index("grp")
    me = lax.axis_index("aux")
    rows, chunks = raw.shape[0], raw.shape[2] // width
    aux_rows = metric.shape[0]
    nvirt = vrow.shape[1]
    relay = n == 4
    steps = plan.shape[0]

    def aux_at(d):
        return lax.rem(me + d, shards)

    if relay:
        one = grp + 1 - 2 * lax.rem(grp, 2)
        two = lax.rem(grp + 2, 4)
        target = [grp, one, two, lax.rem(one + 2, 4)]
        source = target
    else:
        target = [lax.rem(grp + d, n) for d in range(n)]
        source = [lax.rem(grp + n - d, n) for d in range(n)]

    def raw_copy(k):
        part = pl.ds(k * width, width)
        return pltpu.make_async_copy(raw.at[:, :, part], held.at[k], raw_sem.at[k])

    for k in range(chunks):
        raw_copy(k).start()
    load = pltpu.make_async_copy(metric, mvm, msem)
    load.start()

    barrier = pltpu.get_barrier_semaphore()

    @pl.loop(1, shards)
    def _(d):
        pl.semaphore_signal(barrier, inc=1, device_id=(grp, aux_at(d)), device_id_type=MESH)

    for d in range(1, n):
        pl.semaphore_signal(barrier, inc=1, device_id=(target[d], me), device_id_type=MESH)
    pl.semaphore_wait(barrier, shards - 1 + n - 1)

    def in_copy(k, d):
        return pltpu.make_async_remote_copy(
            src_ref=x.at[aux_at(d), k], dst_ref=recv.at[k, me], send_sem=in_send.at[k, d],
            recv_sem=in_recv.at[k, d], device_id=(grp, aux_at(d)), device_id_type=MESH)

    def in_own(k):
        return pltpu.make_async_copy(x.at[me, k], recv.at[k, me], in_local.at[k])

    parity = lax.rem(me, 2)
    per_class = shards // 2

    def class_loop(odd, act):
        @pl.loop(0, per_class)
        def _(e):
            d = 2 * lax.rem(e + per_class // 2, per_class) + (1 - parity if odd else parity)

            @pl.when(d != 0)
            def _():
                act(d)

    def send_step(i):
        class_loop(i // chunks, lambda d: in_copy(i % chunks, d).start())

    def send_after(k):
        class_loop(0, lambda d: in_copy(k, d).wait_send())
        for i in range(k + WINDOW, 2 * chunks if k == chunks - 1 else k + WINDOW + 1):
            send_step(i)

    def wait_in(k):
        in_own(k).wait()

        @pl.loop(1, shards)
        def _(d):
            place = lax.rem(me + shards - d, shards)
            pltpu.make_async_remote_copy(
                src_ref=x.at[place, k], dst_ref=recv.at[k, place], send_sem=in_send.at[k, d],
                recv_sem=in_recv.at[k, d], device_id=(grp, aux_at(d)), device_id_type=MESH).wait_recv()

    def g_copy(k, d):
        return pltpu.make_async_remote_copy(
            src_ref=blocks.at[0, k], dst_ref=blocks.at[d, k], send_sem=g_send.at[d, k],
            recv_sem=g_recv.at[d, k], device_id=(target[d], me), device_id_type=MESH)

    half = aux_rows // 2

    def f_copy(k, way):
        part = pl.ds(way * half, half)
        return pltpu.make_async_remote_copy(
            src_ref=blocks.at[1 + way, k, part], dst_ref=blocks.at[3, k, part], send_sem=f_send.at[way, k],
            recv_sem=f_recv.at[way, k], device_id=(target[2 - way], me), device_id_type=MESH)

    direct = (1, 2) if relay else tuple(range(1, n))

    def forward(k):
        for d in (1, 2):
            g_copy(k, d).wait_recv()
            f_copy(k, d - 1).start()

    tile = min(512, aux_rows)
    for k in range(chunks):
        raw_copy(k).wait()
        x[:, k] = jnp.swapaxes(held[k].astype(jnp.float32), 0, 1).astype(jnp.bfloat16)
        if k < WINDOW:
            send_step(k)
        in_own(k).start()
    vsum[...] = vrow[...] + jnp.broadcast_to(vrow[...], (nvirt, nvirt)).T

    @pl.when(parity == 1)
    def _():
        for k in range(chunks):
            send_after(k)

    for k in range(chunks):
        wait_in(k)

        @pl.when(parity == 0)
        def _():
            send_after(k)

        if k == 0:
            load.wait()

        @pl.loop(0, aux_rows // tile)
        def _(t):
            at = pl.ds(pl.multiple_of(t * tile, tile), tile)
            part = dot(mvm[at, :], recv[k].reshape(aux_rows, width))
            blocks[0, k, at, :] = part.astype(jnp.bfloat16)

        for d in direct:
            g_copy(k, d).start()
        if relay and k >= 1:
            forward(k - 1)
        own_t[k * width:(k + 1) * width, :] = blocks[0, k].T

    def pair(d):
        per = max(1, min(256 // width, chunks))
        for k in range(0, chunks, per):
            right = jnp.concatenate([blocks[d, k + m] for m in range(per)], axis=1)
            exch[:, k * width:(k + per) * width] = dot(own_t[...], right)
        weight = jnp.float32(0.0)
        for s in range(steps):
            weight = weight + jnp.where(plan[s, me] == source[d], jnp.float32(1.0), jnp.float32(0.0))
        shift = occ[grp * shards + me] + occ[source[d] * shards + me]
        value = exch[...]
        below = shift - vsum[...]
        value = weight * ((2.0 * value.T - value) / below)
        amp[d * nvirt:(d + 1) * nvirt, :] = value.astype(jnp.bfloat16)

    pair(0)
    if relay:
        forward(chunks - 1)
        pair(1)
        pair(2)
        for k in range(chunks):
            for way in (0, 1):
                f_copy(k, way).wait_recv()
        pair(3)
    else:
        for d in direct:
            for k in range(chunks):
                g_copy(k, d).wait_recv()
            pair(d)

    def density(d):
        at = pl.ds(pl.multiple_of(aux_at(d) * rows, rows), rows)
        left = jnp.concatenate([blocks[s, k, at, :] for s in range(n) for k in range(chunks)], axis=1)
        dens[d] = dot(left, amp[...]).astype(jnp.bfloat16)

    def out_copy(d):
        return pltpu.make_async_remote_copy(
            src_ref=dens.at[d], dst_ref=y.at[me], send_sem=out_send.at[d], recv_sem=out_recv.at[d],
            device_id=(grp, aux_at(d)), device_id_type=MESH)

    @pl.loop(0, shards - 1)
    def _(t):
        d = 1 + lax.rem(t + shards // 2 - 1, shards - 1)
        density(d)
        out_copy(d).start()

    density(0)
    own_out = pltpu.make_async_copy(dens.at[0], y.at[me], out_local)
    own_out.start()
    own_out.wait()

    for k in range(chunks):
        class_loop(1, lambda d: in_copy(k, d).wait_send())
        for d in direct:
            g_copy(k, d).wait_send()
        if relay:
            for way in (0, 1):
                f_copy(k, way).wait_send()

    @pl.loop(1, shards)
    def _(d):
        place = lax.rem(me + shards - d, shards)
        out_copy(d).wait_send()
        pltpu.make_async_remote_copy(
            src_ref=dens.at[d], dst_ref=y.at[place], send_sem=out_send.at[d], recv_sem=out_recv.at[d],
            device_id=(grp, aux_at(d)), device_id_type=MESH).wait_recv()


def body(integrals, metric, occupied_energy, virtual_energy, plan):
    n, shards = lax.axis_size("grp"), lax.axis_size("aux")
    rows, places, nvirt = integrals.shape
    aux_rows = metric.shape[0]
    width = CHUNK if nvirt % CHUNK == 0 else nvirt
    chunks = nvirt // width
    any_space = pl.BlockSpec(memory_space=pl.ANY)
    vmem = pl.BlockSpec(memory_space=pltpu.VMEM)
    smem = pl.BlockSpec(memory_space=pltpu.SMEM)
    dma = pltpu.SemaphoreType.DMA
    flops = 2 * aux_rows * nvirt * (aux_rows + 2 * n * nvirt)
    y = pl.pallas_call(
        functools.partial(kernel, n, shards, width),
        out_shape=jax.ShapeDtypeStruct((shards, rows, nvirt), jnp.bfloat16),
        in_specs=[any_space, any_space, vmem, smem, smem],
        out_specs=any_space,
        scratch_shapes=[
            pltpu.VMEM((chunks, rows, shards, width), jnp.bfloat16),
            pltpu.VMEM((shards, chunks, rows, width), jnp.bfloat16),
            pltpu.VMEM((aux_rows, aux_rows), jnp.bfloat16),
            pltpu.VMEM((chunks, shards, rows, width), jnp.bfloat16),
            pltpu.VMEM((n, chunks, aux_rows, width), jnp.bfloat16),
            pltpu.VMEM((nvirt, aux_rows), jnp.bfloat16),
            pltpu.VMEM((nvirt, nvirt), jnp.float32),
            pltpu.VMEM((nvirt, nvirt), jnp.float32),
            pltpu.VMEM((n * nvirt, nvirt), jnp.bfloat16),
            pltpu.VMEM((shards, rows, nvirt), jnp.bfloat16),
            dma, dma((chunks,)), dma((chunks, shards)), dma((chunks, shards)), dma((chunks,)),
            dma((n, chunks)), dma((n, chunks)), dma((2, chunks)), dma((2, chunks)),
            dma((shards,)), dma((shards,)), dma,
        ],
        compiler_params=pltpu.CompilerParams(
            collective_id=0, has_side_effects=True, vmem_limit_bytes=56 * 1024 * 1024),
        cost_estimate=pl.CostEstimate(
            flops=flops, bytes_accessed=2 * aux_rows * aux_rows, transcendentals=0),
    )(integrals, metric, virtual_energy.reshape(1, nvirt), occupied_energy, plan)
    return y.transpose(1, 0, 2)


def solution(mesh):
    in_specs = (P("aux", "grp", None), P(), P(), P(), P())
    out_specs = P("aux", "grp", None)
    return jax.shard_map(body, mesh=mesh, in_specs=in_specs, out_specs=out_specs, check_vma=False)
```

```python
import functools

import jax
import jax.numpy as jnp
from jax import lax
from jax.experimental import pallas as pl
from jax.experimental.pallas import tpu as pltpu
from jax.sharding import PartitionSpec as P

MESH = pl.DeviceIdType.MESH
CHUNK = 128
WINDOW = 3


def dot(left, right):
    return lax.dot_general(left, right, (((1,), (0,)), ((), ())), preferred_element_type=jnp.float32)


def kernel(n, shards, width, raw, metric, vrow, occ, plan, y, held, x, mvm, recv, blocks, own_t, exch, vsum, amp, dens,
           msem, raw_sem, in_send, in_recv, in_local, g_send, g_recv, f_send, f_recv, out_send, out_recv, out_local):
    grp = lax.axis_index("grp")
    me = lax.axis_index("aux")
    rows, chunks = raw.shape[0], raw.shape[2] // width
    aux_rows = metric.shape[0]
    nvirt = vrow.shape[1]
    relay = n == 4
    steps = plan.shape[0]

    def aux_at(d):
        return lax.rem(me + d, shards)

    if relay:
        one = grp + 1 - 2 * lax.rem(grp, 2)
        two = lax.rem(grp + 2, 4)
        target = [grp, one, two, lax.rem(one + 2, 4)]
        source = target
    else:
        target = [lax.rem(grp + d, n) for d in range(n)]
        source = [lax.rem(grp + n - d, n) for d in range(n)]

    def raw_copy(k):
        part = pl.ds(k * width, width)
        return pltpu.make_async_copy(raw.at[:, :, part], held.at[k], raw_sem.at[k])

    for k in range(chunks):
        raw_copy(k).start()
    load = pltpu.make_async_copy(metric, mvm, msem)
    load.start()

    barrier = pltpu.get_barrier_semaphore()

    @pl.loop(1, shards)
    def _(d):
        pl.semaphore_signal(barrier, inc=1, device_id=(grp, aux_at(d)), device_id_type=MESH)

    for d in range(1, n):
        pl.semaphore_signal(barrier, inc=1, device_id=(target[d], me), device_id_type=MESH)
    pl.semaphore_wait(barrier, shards - 1 + n - 1)

    def in_copy(k, d):
        return pltpu.make_async_remote_copy(
            src_ref=x.at[aux_at(d), k], dst_ref=recv.at[k, me], send_sem=in_send.at[k, d],
            recv_sem=in_recv.at[k, d], device_id=(grp, aux_at(d)), device_id_type=MESH)

    def in_own(k):
        return pltpu.make_async_copy(x.at[me, k], recv.at[k, me], in_local.at[k])

    parity = lax.rem(me, 2)
    per_class = shards // 2

    def class_loop(odd, act):
        @pl.loop(0, per_class)
        def _(e):
            d = 2 * lax.rem(e + per_class // 2, per_class) + (1 - parity if odd else parity)

            @pl.when(d != 0)
            def _():
                act(d)

    def send_step(i):
        class_loop(i // chunks, lambda d: in_copy(i % chunks, d).start())

    def send_after(k):
        class_loop(0, lambda d: in_copy(k, d).wait_send())
        for i in range(k + WINDOW, 2 * chunks if k == chunks - 1 else k + WINDOW + 1):
            send_step(i)

    def wait_in(k):
        in_own(k).wait()

        @pl.loop(1, shards)
        def _(d):
            place = lax.rem(me + shards - d, shards)
            pltpu.make_async_remote_copy(
                src_ref=x.at[place, k], dst_ref=recv.at[k, place], send_sem=in_send.at[k, d],
                recv_sem=in_recv.at[k, d], device_id=(grp, aux_at(d)), device_id_type=MESH).wait_recv()

    def g_copy(k, d):
        return pltpu.make_async_remote_copy(
            src_ref=blocks.at[0, k], dst_ref=blocks.at[d, k], send_sem=g_send.at[d, k],
            recv_sem=g_recv.at[d, k], device_id=(target[d], me), device_id_type=MESH)

    half = aux_rows // 2

    def f_copy(k, way):
        part = pl.ds(way * half, half)
        return pltpu.make_async_remote_copy(
            src_ref=blocks.at[1 + way, k, part], dst_ref=blocks.at[3, k, part], send_sem=f_send.at[way, k],
            recv_sem=f_recv.at[way, k], device_id=(target[2 - way], me), device_id_type=MESH)

    direct = (1, 2) if relay else tuple(range(1, n))

    def forward(k):
        for d in (1, 2):
            g_copy(k, d).wait_recv()
            f_copy(k, d - 1).start()

    tile = min(512, aux_rows)
    for k in range(chunks):
        raw_copy(k).wait()
        x[:, k] = jnp.swapaxes(held[k].astype(jnp.float32), 0, 1).astype(jnp.bfloat16)
        if k < WINDOW:
            send_step(k)
        in_own(k).start()
    vsum[...] = vrow[...] + jnp.broadcast_to(vrow[...], (nvirt, nvirt)).T

    @pl.when(parity == 1)
    def _():
        for k in range(chunks):
            send_after(k)

    for k in range(chunks):
        wait_in(k)

        @pl.when(parity == 0)
        def _():
            send_after(k)

        if k == 0:
            load.wait()

        @pl.loop(0, aux_rows // tile)
        def _(t):
            at = pl.ds(pl.multiple_of(t * tile, tile), tile)
            part = dot(mvm[at, :], recv[k].reshape(aux_rows, width))
            blocks[0, k, at, :] = part.astype(jnp.bfloat16)

        for d in direct:
            g_copy(k, d).start()
        if relay and k >= 1:
            forward(k - 1)
        own_t[k * width:(k + 1) * width, :] = blocks[0, k].T

    def pair(d, ready=lambda k: None):
        per = max(1, min(256 // width, chunks))
        for k in range(0, chunks, per):
            for m in range(per):
                ready(k + m)
            right = jnp.concatenate([blocks[d, k + m] for m in range(per)], axis=1)
            exch[:, k * width:(k + per) * width] = dot(own_t[...], right)
        weight = jnp.float32(0.0)
        for s in range(steps):
            weight = weight + jnp.where(plan[s, me] == source[d], jnp.float32(1.0), jnp.float32(0.0))
        shift = occ[grp * shards + me] + occ[source[d] * shards + me]
        value = exch[...]
        below = shift - vsum[...]
        value = weight * ((2.0 * value.T - value) / below)
        amp[d * nvirt:(d + 1) * nvirt, :] = value.astype(jnp.bfloat16)

    pair(0)
    if relay:
        forward(chunks - 1)
        pair(1)
        pair(2)

        def ready(k):
            for way in (0, 1):
                f_copy(k, way).wait_recv()

        pair(3, ready)
    else:
        for d in direct:
            for k in range(chunks):
                g_copy(k, d).wait_recv()
            pair(d)

    def density(d):
        at = pl.ds(pl.multiple_of(aux_at(d) * rows, rows), rows)
        left = jnp.concatenate([blocks[s, k, at, :] for s in range(n) for k in range(chunks)], axis=1)
        dens[d] = dot(left, amp[...]).astype(jnp.bfloat16)

    def out_copy(d):
        return pltpu.make_async_remote_copy(
            src_ref=dens.at[d], dst_ref=y.at[me], send_sem=out_send.at[d], recv_sem=out_recv.at[d],
            device_id=(grp, aux_at(d)), device_id_type=MESH)

    @pl.loop(0, shards - 1)
    def _(t):
        d = 1 + lax.rem(t + shards // 2 - 1, shards - 1)
        density(d)
        out_copy(d).start()

    density(0)
    own_out = pltpu.make_async_copy(dens.at[0], y.at[me], out_local)
    own_out.start()
    own_out.wait()

    for k in range(chunks):
        class_loop(1, lambda d: in_copy(k, d).wait_send())
        for d in direct:
            g_copy(k, d).wait_send()
        if relay:
            for way in (0, 1):
                f_copy(k, way).wait_send()

    @pl.loop(1, shards)
    def _(d):
        place = lax.rem(me + shards - d, shards)
        out_copy(d).wait_send()
        pltpu.make_async_remote_copy(
            src_ref=dens.at[d], dst_ref=y.at[place], send_sem=out_send.at[d], recv_sem=out_recv.at[d],
            device_id=(grp, aux_at(d)), device_id_type=MESH).wait_recv()


def body(integrals, metric, occupied_energy, virtual_energy, plan):
    n, shards = lax.axis_size("grp"), lax.axis_size("aux")
    rows, places, nvirt = integrals.shape
    aux_rows = metric.shape[0]
    width = CHUNK if nvirt % CHUNK == 0 else nvirt
    chunks = nvirt // width
    any_space = pl.BlockSpec(memory_space=pl.ANY)
    vmem = pl.BlockSpec(memory_space=pltpu.VMEM)
    smem = pl.BlockSpec(memory_space=pltpu.SMEM)
    dma = pltpu.SemaphoreType.DMA
    flops = 2 * aux_rows * nvirt * (aux_rows + 2 * n * nvirt)
    y = pl.pallas_call(
        functools.partial(kernel, n, shards, width),
        out_shape=jax.ShapeDtypeStruct((shards, rows, nvirt), jnp.bfloat16),
        in_specs=[any_space, any_space, vmem, smem, smem],
        out_specs=any_space,
        scratch_shapes=[
            pltpu.VMEM((chunks, rows, shards, width), jnp.bfloat16),
            pltpu.VMEM((shards, chunks, rows, width), jnp.bfloat16),
            pltpu.VMEM((aux_rows, aux_rows), jnp.bfloat16),
            pltpu.VMEM((chunks, shards, rows, width), jnp.bfloat16),
            pltpu.VMEM((n, chunks, aux_rows, width), jnp.bfloat16),
            pltpu.VMEM((nvirt, aux_rows), jnp.bfloat16),
            pltpu.VMEM((nvirt, nvirt), jnp.float32),
            pltpu.VMEM((nvirt, nvirt), jnp.float32),
            pltpu.VMEM((n * nvirt, nvirt), jnp.bfloat16),
            pltpu.VMEM((shards, rows, nvirt), jnp.bfloat16),
            dma, dma((chunks,)), dma((chunks, shards)), dma((chunks, shards)), dma((chunks,)),
            dma((n, chunks)), dma((n, chunks)), dma((2, chunks)), dma((2, chunks)),
            dma((shards,)), dma((shards,)), dma,
        ],
        compiler_params=pltpu.CompilerParams(
            collective_id=0, has_side_effects=True, vmem_limit_bytes=56 * 1024 * 1024),
        cost_estimate=pl.CostEstimate(
            flops=flops, bytes_accessed=2 * aux_rows * aux_rows, transcendentals=0),
    )(integrals, metric, virtual_energy.reshape(1, nvirt), occupied_energy, plan)
    return y.transpose(1, 0, 2)


def solution(mesh):
    in_specs = (P("aux", "grp", None), P(), P(), P(), P())
    out_specs = P("aux", "grp", None)
    return jax.shard_map(body, mesh=mesh, in_specs=in_specs, out_specs=out_specs, check_vma=False)
```

```python
import functools

import jax
import jax.numpy as jnp
from jax import lax
from jax.experimental import pallas as pl
from jax.experimental.pallas import tpu as pltpu
from jax.sharding import PartitionSpec as P

MESH = pl.DeviceIdType.MESH
CHUNK = 128
WINDOW = 4


def dot(left, right):
    return lax.dot_general(left, right, (((1,), (0,)), ((), ())), preferred_element_type=jnp.float32)


def kernel(n, shards, width, raw, metric, vrow, occ, plan, y, held, x, mvm, recv, blocks, own_t, exch, vsum, amp, dens,
           msem, raw_sem, in_send, in_recv, in_local, g_send, g_recv, f_send, f_recv, out_send, out_recv, out_local):
    grp = lax.axis_index("grp")
    me = lax.axis_index("aux")
    rows, chunks = raw.shape[0], raw.shape[2] // width
    aux_rows = metric.shape[0]
    nvirt = vrow.shape[1]
    relay = n == 4
    steps = plan.shape[0]

    def aux_at(d):
        return lax.rem(me + d, shards)

    if relay:
        one = grp + 1 - 2 * lax.rem(grp, 2)
        two = lax.rem(grp + 2, 4)
        target = [grp, one, two, lax.rem(one + 2, 4)]
        source = target
    else:
        target = [lax.rem(grp + d, n) for d in range(n)]
        source = [lax.rem(grp + n - d, n) for d in range(n)]

    def raw_copy(k):
        part = pl.ds(k * width, width)
        return pltpu.make_async_copy(raw.at[:, :, part], held.at[k], raw_sem.at[k])

    for k in range(chunks):
        raw_copy(k).start()
    load = pltpu.make_async_copy(metric, mvm, msem)
    load.start()

    barrier = pltpu.get_barrier_semaphore()

    @pl.loop(1, shards)
    def _(d):
        pl.semaphore_signal(barrier, inc=1, device_id=(grp, aux_at(d)), device_id_type=MESH)

    for d in range(1, n):
        pl.semaphore_signal(barrier, inc=1, device_id=(target[d], me), device_id_type=MESH)
    pl.semaphore_wait(barrier, shards - 1 + n - 1)

    def in_copy(k, d):
        return pltpu.make_async_remote_copy(
            src_ref=x.at[aux_at(d), k], dst_ref=recv.at[k, me], send_sem=in_send.at[k, d],
            recv_sem=in_recv.at[k, d], device_id=(grp, aux_at(d)), device_id_type=MESH)

    def in_own(k):
        return pltpu.make_async_copy(x.at[me, k], recv.at[k, me], in_local.at[k])

    parity = lax.rem(me, 2)
    per_class = shards // 2

    def class_loop(odd, act):
        @pl.loop(0, per_class)
        def _(e):
            d = 2 * lax.rem(e + per_class // 2, per_class) + (1 - parity if odd else parity)

            @pl.when(d != 0)
            def _():
                act(d)

    def send_step(i):
        class_loop(i // chunks, lambda d: in_copy(i % chunks, d).start())

    def send_after(k):
        class_loop(0, lambda d: in_copy(k, d).wait_send())
        for i in range(k + WINDOW, 2 * chunks if k == chunks - 1 else k + WINDOW + 1):
            send_step(i)

    def wait_in(k):
        in_own(k).wait()

        @pl.loop(1, shards)
        def _(d):
            place = lax.rem(me + shards - d, shards)
            pltpu.make_async_remote_copy(
                src_ref=x.at[place, k], dst_ref=recv.at[k, place], send_sem=in_send.at[k, d],
                recv_sem=in_recv.at[k, d], device_id=(grp, aux_at(d)), device_id_type=MESH).wait_recv()

    def g_copy(k, d):
        return pltpu.make_async_remote_copy(
            src_ref=blocks.at[0, k], dst_ref=blocks.at[d, k], send_sem=g_send.at[d, k],
            recv_sem=g_recv.at[d, k], device_id=(target[d], me), device_id_type=MESH)

    half = aux_rows // 2

    def f_copy(k, way):
        part = pl.ds(way * half, half)
        return pltpu.make_async_remote_copy(
            src_ref=blocks.at[1 + way, k, part], dst_ref=blocks.at[3, k, part], send_sem=f_send.at[way, k],
            recv_sem=f_recv.at[way, k], device_id=(target[2 - way], me), device_id_type=MESH)

    direct = (1, 2) if relay else tuple(range(1, n))

    def forward(k):
        for d in (1, 2):
            g_copy(k, d).wait_recv()
            f_copy(k, d - 1).start()

    tile = min(512, aux_rows)
    for k in range(chunks):
        raw_copy(k).wait()
        x[:, k] = jnp.swapaxes(held[k].astype(jnp.float32), 0, 1).astype(jnp.bfloat16)
        if k < WINDOW:
            send_step(k)
        in_own(k).start()
    vsum[...] = vrow[...] + jnp.broadcast_to(vrow[...], (nvirt, nvirt)).T

    @pl.when(parity == 1)
    def _():
        for k in range(chunks):
            send_after(k)

    for k in range(chunks):
        wait_in(k)

        @pl.when(parity == 0)
        def _():
            send_after(k)

        if k == 0:
            load.wait()

        @pl.loop(0, aux_rows // tile)
        def _(t):
            at = pl.ds(pl.multiple_of(t * tile, tile), tile)
            part = dot(mvm[at, :], recv[k].reshape(aux_rows, width))
            blocks[0, k, at, :] = part.astype(jnp.bfloat16)

        for d in direct:
            g_copy(k, d).start()
        if relay and k >= 1:
            forward(k - 1)
        own_t[k * width:(k + 1) * width, :] = blocks[0, k].T

    def pair(d, ready=lambda k: None):
        per = max(1, min(256 // width, chunks))
        for k in range(0, chunks, per):
            for m in range(per):
                ready(k + m)
            right = jnp.concatenate([blocks[d, k + m] for m in range(per)], axis=1)
            exch[:, k * width:(k + per) * width] = dot(own_t[...], right)
        weight = jnp.float32(0.0)
        for s in range(steps):
            weight = weight + jnp.where(plan[s, me] == source[d], jnp.float32(1.0), jnp.float32(0.0))
        shift = occ[grp * shards + me] + occ[source[d] * shards + me]
        value = exch[...]
        below = shift - vsum[...]
        value = weight * ((2.0 * value.T - value) / below)
        amp[d * nvirt:(d + 1) * nvirt, :] = value.astype(jnp.bfloat16)

    pair(0)
    if relay:
        forward(chunks - 1)
        pair(1)
        pair(2)

        def ready(k):
            for way in (0, 1):
                f_copy(k, way).wait_recv()

        pair(3, ready)
    else:
        for d in direct:
            for k in range(chunks):
                g_copy(k, d).wait_recv()
            pair(d)

    def density(d):
        at = pl.ds(pl.multiple_of(aux_at(d) * rows, rows), rows)
        left = jnp.concatenate([blocks[s, k, at, :] for s in range(n) for k in range(chunks)], axis=1)
        dens[d] = dot(left, amp[...]).astype(jnp.bfloat16)

    def out_copy(d):
        return pltpu.make_async_remote_copy(
            src_ref=dens.at[d], dst_ref=y.at[me], send_sem=out_send.at[d], recv_sem=out_recv.at[d],
            device_id=(grp, aux_at(d)), device_id_type=MESH)

    @pl.loop(0, shards - 1)
    def _(t):
        d = 1 + lax.rem(t + shards // 2 - 1, shards - 1)
        density(d)
        out_copy(d).start()

    density(0)
    own_out = pltpu.make_async_copy(dens.at[0], y.at[me], out_local)
    own_out.start()
    own_out.wait()

    for k in range(chunks):
        class_loop(1, lambda d: in_copy(k, d).wait_send())
        for d in direct:
            g_copy(k, d).wait_send()
        if relay:
            for way in (0, 1):
                f_copy(k, way).wait_send()

    @pl.loop(1, shards)
    def _(d):
        place = lax.rem(me + shards - d, shards)
        out_copy(d).wait_send()
        pltpu.make_async_remote_copy(
            src_ref=dens.at[d], dst_ref=y.at[place], send_sem=out_send.at[d], recv_sem=out_recv.at[d],
            device_id=(grp, aux_at(d)), device_id_type=MESH).wait_recv()


def body(integrals, metric, occupied_energy, virtual_energy, plan):
    n, shards = lax.axis_size("grp"), lax.axis_size("aux")
    rows, places, nvirt = integrals.shape
    aux_rows = metric.shape[0]
    width = CHUNK if nvirt % CHUNK == 0 else nvirt
    chunks = nvirt // width
    any_space = pl.BlockSpec(memory_space=pl.ANY)
    vmem = pl.BlockSpec(memory_space=pltpu.VMEM)
    smem = pl.BlockSpec(memory_space=pltpu.SMEM)
    dma = pltpu.SemaphoreType.DMA
    flops = 2 * aux_rows * nvirt * (aux_rows + 2 * n * nvirt)
    y = pl.pallas_call(
        functools.partial(kernel, n, shards, width),
        out_shape=jax.ShapeDtypeStruct((shards, rows, nvirt), jnp.bfloat16),
        in_specs=[any_space, any_space, vmem, smem, smem],
        out_specs=any_space,
        scratch_shapes=[
            pltpu.VMEM((chunks, rows, shards, width), jnp.bfloat16),
            pltpu.VMEM((shards, chunks, rows, width), jnp.bfloat16),
            pltpu.VMEM((aux_rows, aux_rows), jnp.bfloat16),
            pltpu.VMEM((chunks, shards, rows, width), jnp.bfloat16),
            pltpu.VMEM((n, chunks, aux_rows, width), jnp.bfloat16),
            pltpu.VMEM((nvirt, aux_rows), jnp.bfloat16),
            pltpu.VMEM((nvirt, nvirt), jnp.float32),
            pltpu.VMEM((nvirt, nvirt), jnp.float32),
            pltpu.VMEM((n * nvirt, nvirt), jnp.bfloat16),
            pltpu.VMEM((shards, rows, nvirt), jnp.bfloat16),
            dma, dma((chunks,)), dma((chunks, shards)), dma((chunks, shards)), dma((chunks,)),
            dma((n, chunks)), dma((n, chunks)), dma((2, chunks)), dma((2, chunks)),
            dma((shards,)), dma((shards,)), dma,
        ],
        compiler_params=pltpu.CompilerParams(
            collective_id=0, has_side_effects=True, vmem_limit_bytes=56 * 1024 * 1024),
        cost_estimate=pl.CostEstimate(
            flops=flops, bytes_accessed=2 * aux_rows * aux_rows, transcendentals=0),
    )(integrals, metric, virtual_energy.reshape(1, nvirt), occupied_energy, plan)
    return y.transpose(1, 0, 2)


def solution(mesh):
    in_specs = (P("aux", "grp", None), P(), P(), P(), P())
    out_specs = P("aux", "grp", None)
    return jax.shard_map(body, mesh=mesh, in_specs=in_specs, out_specs=out_specs, check_vma=False)
```
